512 devices in a mesh: outer: 16 (over x, y_lo, core), inner: 32 (over y_hi, z).
Axes of the slice: x: 4, y: 4 (y_hi: 2, y_lo: 2; y = y_hi * 2 + y_lo), z: 16, core: 2. Of those that a mesh axis runs over, the one named last changes fastest.
Arguments:
- queries: bfloat16 [262144, 1024], P(('outer', 'inner')), may hold values from -1000 to 1000
- kv_codes: bfloat16 [262144, 256], P(('outer', 'inner')), may hold values from -4 to 4
- scale_exp: int32 [2048, 2], P(('outer', 'inner')), may hold values from -1 to 1
- positions: int32 [262144], P(('outer', 'inner')), may hold values from 0 to 262143, as said below
Outputs:
- attended: bfloat16 [262144, 1024], P(('outer', 'inner'))
The draws below stay inside these ranges and needn't reach their ends.
Inputs may be any that keep to these rules, and one draw needn't show every extreme that they name: Every position occurs once; each block of 512 rows is two runs of 256 rows holding consecutive rising positions, each run starting at a multiple of 256.
All inputs are finite; a program needn't handle non-finite values.
Results may differ from the reference program's by a relative error of at most 0.0065.
Values may be sent and summed in bfloat16 or wider, within the bound.
A program may use at most 64 MiB of HBM per device.

```python
import jax
import jax.numpy as jnp
from jax import lax

HEADS = 8
HEAD_DIM = 128
TOK_DEV = 512
SCALE_ROWS = 128
SPAN = 256
TOKENS = 262144
N_OUTER = 16
N_INNER = 32


def code_rows(key):
    base = jnp.clip(jax.random.normal(key, (TOKENS, 2 * HEAD_DIM), jnp.float32), -3.9, 3.9)
    following = jnp.roll(base, -1, axis=0)
    near = jnp.clip(following, -3.9, 3.9)
    row_sel = (jnp.arange(TOKENS) % 8 == 4)[:, None]
    col_sel = (jnp.arange(2 * HEAD_DIM) < HEAD_DIM)[None, :]
    return jnp.where(row_sel & col_sel, near, base)


def draw_kv_codes(key, part):
    codes = code_rows(key)
    return codes.astype(jnp.bfloat16)


def draw_queries(key, part):
    key = jax.random.fold_in(key, 5)
    full = jnp.clip(jax.random.normal(key, (TOKENS, HEADS, HEAD_DIM), jnp.float32), -6.0, 6.0)
    return full.reshape(TOKENS, HEADS * HEAD_DIM).astype(jnp.bfloat16)


def draw_positions(key, part):
    key = jax.random.fold_in(key, 9)
    order = jax.random.permutation(key, TOKENS // SPAN).astype(jnp.int32)
    return (order[:, None] * SPAN + jnp.arange(SPAN, dtype=jnp.int32)[None, :]).reshape(TOKENS)


def with_ends(values, stream_key, least, top_value):
    longest = values.shape.index(max(values.shape))
    spots = []
    for shift in (0, 1):
        where = [jax.random.randint(jax.random.fold_in(stream_key, axis), (), 0, length) for axis, length in enumerate(values.shape)]
        where[longest] = (where[longest] + shift) % values.shape[longest]
        spots.append(tuple(where))
    return values.at[spots[0]].set(least).at[spots[1]].set(top_value)


def setup_inputs(seed: int = 0) -> dict:
    splits = jax.random.split(jax.random.key(seed), 5)
    queries = draw_queries(jax.random.fold_in(splits[4], 71), 0)
    kv_codes = draw_kv_codes(jax.random.fold_in(splits[4], 71), 0)
    scale_exp = with_ends(jax.random.randint(splits[2], (TOKENS // SCALE_ROWS, 2), -1, 2), jax.random.fold_in(splits[2], 1), -1, 1).astype(jnp.int32)
    positions = draw_positions(jax.random.fold_in(splits[4], 71), 0)
    return {"queries": queries, "kv_codes": kv_codes, "scale_exp": scale_exp, "positions": positions}


def reference(queries, kv_codes, scale_exp, positions):
    blocks = N_OUTER * N_INNER
    query_blocks = queries.reshape(blocks, TOK_DEV, HEADS, HEAD_DIM)
    code_blocks = kv_codes.reshape(blocks, TOK_DEV, 2 * HEAD_DIM)
    exp_blocks = scale_exp.reshape(blocks, TOK_DEV // SCALE_ROWS, 2)
    pos_blocks = positions.reshape(blocks, TOK_DEV)
    factor = HEAD_DIM ** -0.5

    def one_block(index):
        outer_idx = index // N_INNER
        inner_idx = index % N_INNER
        sources = jnp.stack([outer_idx * N_INNER + (inner_idx - 0) % N_INNER,
                             outer_idx * N_INNER + (inner_idx - 1) % N_INNER,
                             outer_idx * N_INNER + (inner_idx - 2) % N_INNER,
                             outer_idx * N_INNER + (inner_idx - 3) % N_INNER,
                             ((outer_idx - 1) % N_OUTER) * N_INNER + inner_idx]).astype(jnp.int32)
        codes = code_blocks[sources].astype(jnp.float32)
        scales = jnp.exp2(exp_blocks[sources].astype(jnp.float32))
        scales = jnp.repeat(scales, SCALE_ROWS, axis=1)
        keys = (codes[:, :, :HEAD_DIM] * scales[:, :, 0:1]).astype(jnp.bfloat16).reshape(5 * TOK_DEV, HEAD_DIM)
        values = (codes[:, :, HEAD_DIM:] * scales[:, :, 1:2]).astype(jnp.bfloat16).reshape(5 * TOK_DEV, HEAD_DIM)
        key_pos = pos_blocks[sources].reshape(5 * TOK_DEV)
        query_pos = pos_blocks[index]
        query_rows = query_blocks[index].astype(jnp.float32)
        scores = jnp.einsum("thd,kd->thk", query_rows, keys.astype(jnp.float32)) * factor
        visible = (key_pos[None, None, :] <= query_pos[:, None, None])
        scores = jnp.where(visible, scores, -1e30)
        top = jnp.max(scores, axis=2, keepdims=True)
        weights = jnp.where(visible, jnp.exp(scores - top), 0.0)
        total = jnp.sum(weights, axis=2)
        rounded = weights.astype(jnp.bfloat16)
        numer = jnp.einsum("thk,kd->thd", rounded.astype(jnp.float32), values.astype(jnp.float32))
        return (numer / total[:, :, None]).astype(jnp.bfloat16)

    result = lax.map(one_block, jnp.arange(blocks, dtype=jnp.int32))
    return result.reshape(TOKENS, HEADS * HEAD_DIM)
```

```python
import functools
import math

import jax
import jax.numpy as jnp
from jax import lax
from jax.experimental import pallas as pl
from jax.experimental.pallas import tpu as pltpu
from jax.sharding import PartitionSpec as P

MESH = pl.DeviceIdType.MESH
HEADS = 8
DIM = 128
SPAN = 256
GROUP = 128
BIG = 1e30
SCALE = math.log2(math.e) / math.sqrt(128.0)
BF16 = jnp.bfloat16
F32 = jnp.float32

FORWARD = {2: 6, 4: 7, 6: 8, 7: 9}
CHUNKS = 10


def kernel(
    n_outer, n_inner,
    q_hbm, kv_hbm, exp_ref, pos_ref, out_hbm,
    q_in, kvb, meta, q2, kt, va, acc, mx, bias, stage,
    local_sem, send_sem, recv_sem, msend_sem, mrecv_sem, out_sem,
):
    o, i = lax.axis_index("outer"), lax.axis_index("inner")
    ahead = (o, lax.rem(i + 1, n_inner))
    behind = (o, lax.rem(i + n_inner - 1, n_inner))
    above = (lax.rem(o + 1, n_outer), i)
    below = (lax.rem(o + n_outer - 1, n_outer), i)

    barrier = pltpu.get_barrier_semaphore()
    for peer in (ahead, behind, above, below):
        pl.semaphore_signal(barrier, inc=1, device_id=peer, device_id_type=MESH)

    q_copy = pltpu.make_async_copy(q_hbm, q_in, local_sem.at[0])
    q_copy.start()
    own = []
    for s in range(2):
        own.append(pltpu.make_async_copy(kv_hbm.at[pl.ds(s * SPAN, SPAN)], kvb.at[s], local_sem.at[1 + s]))
        own[s].start()

    for s in range(2):
        for g in range(2):
            for side in range(2):
                e = jnp.full((1, 128), exp_ref[side, 2 * s + g], jnp.int32)
                f = jnp.where(e > 0, 2.0, jnp.where(e < 0, 0.5, 1.0)).astype(F32)
                meta[s, pl.ds(2 * side + g, 1), :] = f
        meta[s, pl.ds(4, 1), :] = jnp.full((1, 128), pos_ref[s * SPAN], jnp.int32).astype(F32)
        meta[s, pl.ds(5, 3), :] = jnp.zeros((3, 128), F32)

    pl.semaphore_wait(barrier, 4)

    def send(src, meta_src, chunk, device):
        pltpu.make_async_remote_copy(
            src_ref=meta_src, dst_ref=meta.at[chunk], send_sem=msend_sem.at[chunk],
            recv_sem=mrecv_sem.at[chunk], device_id=device, device_id_type=MESH,
        ).start()
        pltpu.make_async_remote_copy(
            src_ref=src, dst_ref=kvb.at[chunk], send_sem=send_sem.at[chunk],
            recv_sem=recv_sem.at[chunk], device_id=device, device_id_type=MESH,
        ).start()

    def arrived(chunk):
        pltpu.make_async_remote_copy(
            src_ref=meta.at[chunk], dst_ref=meta.at[chunk], send_sem=msend_sem.at[chunk],
            recv_sem=mrecv_sem.at[chunk], device_id=ahead, device_id_type=MESH,
        ).wait_recv()
        pltpu.make_async_remote_copy(
            src_ref=kvb.at[chunk], dst_ref=kvb.at[chunk], send_sem=send_sem.at[chunk],
            recv_sem=recv_sem.at[chunk], device_id=ahead, device_id_type=MESH,
        ).wait_recv()

    def sent(chunk):
        pltpu.make_async_remote_copy(
            src_ref=meta.at[chunk], dst_ref=meta.at[chunk], send_sem=msend_sem.at[chunk],
            recv_sem=mrecv_sem.at[chunk], device_id=ahead, device_id_type=MESH,
        ).wait_send()
        pltpu.make_async_remote_copy(
            src_ref=kvb.at[chunk], dst_ref=kvb.at[chunk], send_sem=send_sem.at[chunk],
            recv_sem=recv_sem.at[chunk], device_id=ahead, device_id_type=MESH,
        ).wait_send()

    for s in range(2):
        rows = kv_hbm.at[pl.ds(s * SPAN, SPAN)]
        send(rows, meta.at[s], 2 + 2 * s, ahead)
        send(rows, meta.at[s], 3 + 2 * s, above)

    q_copy.wait()
    for h in range(HEADS):
        x = q_in[:, h * DIM : (h + 1) * DIM].astype(F32) * SCALE
        hi = x.astype(BF16)
        q2[h, :, 0:DIM] = hi
        q2[h, :, DIM : 2 * DIM] = (x - hi.astype(F32)).astype(BF16)
    mx[...] = jnp.full(mx.shape, -BIG, F32)
    acc[...] = jnp.zeros(acc.shape, F32)
    va[:, DIM : 2 * DIM] = jnp.ones((SPAN, DIM), BF16)

    def unpack(chunk):
        for g in range(2):
            rows = pl.ds(g * GROUP, GROUP)
            k = kvb[chunk, rows, 0:DIM].astype(F32) * meta[chunk, pl.ds(g, 1), :]
            k = k.T.astype(BF16)
            kt[0:DIM, g * GROUP : (g + 1) * GROUP] = k
            kt[DIM : 2 * DIM, g * GROUP : (g + 1) * GROUP] = k
            v = kvb[chunk, rows, DIM : 2 * DIM].astype(F32) * meta[chunk, pl.ds(2 + g, 1), :]
            va[rows, 0:DIM] = v.astype(BF16)

    def attend(h, penalty):
        s = jnp.dot(q2[h], kt[...], preferred_element_type=F32)
        if penalty is None:
            s = s + bias[...]
        m_old = mx[h]
        m_new, p = [], []
        for r in range(2):
            rows = slice(r * SPAN, (r + 1) * SPAN)
            a, b = s[rows, 0:128], s[rows, 128:256]
            top = jnp.max(jnp.maximum(a, b), axis=1, keepdims=True)
            if penalty is None:
                m = jnp.maximum(m_old[rows], top)
                off = m
            else:
                m = jnp.maximum(m_old[rows], top - penalty[r])
                off = m + penalty[r]
            m_new.append(m)
            p.append(jnp.concatenate([jnp.exp2(a - off), jnp.exp2(b - off)], axis=1).astype(BF16))
        m_new = jnp.concatenate(m_new, axis=0)
        alpha = jnp.exp2(m_old - m_new)
        add = jnp.dot(jnp.concatenate(p, axis=0), va[...], preferred_element_type=F32)
        numer = acc[h, :, 0:DIM] * alpha + add[:, 0:DIM]
        total = acc[h, :, DIM : 2 * DIM] * alpha + add[:, DIM : 2 * DIM]
        return m_new, numer, total

    def update(penalty):
        for h in range(HEADS):
            m_new, numer, total = attend(h, penalty)
            mx[h] = m_new
            acc[h, :, 0:DIM] = numer
            acc[h, :, DIM : 2 * DIM] = total

    def penalties(chunk):
        key = meta[chunk, pl.ds(4, 1), :]
        return [jnp.where(key < meta[r, pl.ds(4, 1), :], 0.0, BIG) for r in range(2)]

    for s in range(2):
        own[s].wait()

    def own_step(s, carry):
        unpack(s)
        row = lax.broadcasted_iota(jnp.int32, (SPAN, 128), 0)
        col = lax.broadcasted_iota(jnp.int32, (SPAN, 128), 1)
        for r in range(2):
            apart = meta[r, pl.ds(4, 1), :] - meta[s, pl.ds(4, 1), :]
            for c in range(2):
                ahead_by = (row - col - c * 128).astype(F32) + apart
                bias[r * SPAN : (r + 1) * SPAN, c * 128 : (c + 1) * 128] = jnp.where(ahead_by >= 0, 0.0, -BIG)
        update(None)
        return carry

    lax.fori_loop(0, 2, own_step, 0)

    def step(t, carry):
        arrived(t)
        for chunk, later in FORWARD.items():
            @pl.when(t == chunk)
            def _(chunk=chunk, later=later):
                send(kvb.at[chunk], meta.at[chunk], later, ahead)
        unpack(t)
        update(penalties(t))
        return carry

    lax.fori_loop(2, CHUNKS - 1, step, 0)

    last = CHUNKS - 1
    arrived(last)
    unpack(last)
    penalty = penalties(last)
    outs = []
    for h in range(HEADS):
        _, numer, total = attend(h, penalty)
        stage[h] = (numer / total).astype(BF16)
        outs.append(pltpu.make_async_copy(stage.at[h], out_hbm.at[:, pl.ds(h * DIM, DIM)], out_sem.at[h]))
        outs[h].start()
    for chunk in range(2, CHUNKS):
        sent(chunk)
    for copy in outs:
        copy.wait()


def solution(mesh):
    n_outer, n_inner = mesh.shape["outer"], mesh.shape["inner"]

    def local(queries, kv_codes, scale_exp, positions):
        tokens = queries.shape[0]
        anywhere = pl.BlockSpec(memory_space=pl.ANY)
        scalars = pl.BlockSpec(memory_space=pltpu.SMEM)
        return pl.pallas_call(
            functools.partial(kernel, n_outer, n_inner),
            out_shape=jax.ShapeDtypeStruct((tokens, HEADS * DIM), BF16),
            in_specs=[anywhere, anywhere, scalars, scalars],
            out_specs=anywhere,
            scratch_shapes=[
                pltpu.VMEM((tokens, HEADS * DIM), BF16),
                pltpu.VMEM((CHUNKS, SPAN, 2 * DIM), BF16),
                pltpu.VMEM((CHUNKS, 8, 128), F32),
                pltpu.VMEM((HEADS, tokens, 2 * DIM), BF16),
                pltpu.VMEM((2 * DIM, SPAN), BF16),
                pltpu.VMEM((SPAN, 2 * DIM), BF16),
                pltpu.VMEM((HEADS, tokens, 2 * DIM), F32),
                pltpu.VMEM((HEADS, tokens, 128), F32),
                pltpu.VMEM((tokens, SPAN), F32),
                pltpu.VMEM((HEADS, tokens, DIM), BF16),
                pltpu.SemaphoreType.DMA((3,)),
                pltpu.SemaphoreType.DMA((CHUNKS,)),
                pltpu.SemaphoreType.DMA((CHUNKS,)),
                pltpu.SemaphoreType.DMA((CHUNKS,)),
                pltpu.SemaphoreType.DMA((CHUNKS,)),
                pltpu.SemaphoreType.DMA((HEADS,)),
            ],
            compiler_params=pltpu.CompilerParams(
                collective_id=0, has_side_effects=True, vmem_limit_bytes=60 * 2**20
            ),
            name="span_attention",
        )(queries, kv_codes, scale_exp.T, positions)

    split = P(("outer", "inner"), None)
    return jax.shard_map(
        local,
        mesh=mesh,
        in_specs=(split, split, split, P(("outer", "inner"))),
        out_specs=split,
        check_vma=False,
    )
```

```python
import functools
import math

import jax
import jax.numpy as jnp
from jax import lax
from jax.experimental import pallas as pl
from jax.experimental.pallas import tpu as pltpu
from jax.sharding import PartitionSpec as P

MESH = pl.DeviceIdType.MESH
HEADS = 8
DIM = 128
SPAN = 256
GROUP = 128
BIG = 1e30
SCALE = math.log2(math.e) / math.sqrt(128.0)
BF16 = jnp.bfloat16
F32 = jnp.float32

BLOCKS, CHUNKS = 5, 10


def kernel(
    n_outer, n_inner,
    q_hbm, kv_hbm, exp_hbm, pos_hbm, out_ref,
    exp_ref, pos_ref, q_in, kvb, notes, q2, kt, va, acc, mx, bias,
    local_sem, send_sem, recv_sem, note_send, note_recv,
):
    o, i = lax.axis_index("outer"), lax.axis_index("inner")
    z = lax.rem(i, 16)
    ahead = (o, lax.rem(i + 1, n_inner))
    behind = (o, lax.rem(i + n_inner - 1, n_inner))
    above = (lax.rem(o + 1, n_outer), i)
    below = (lax.rem(o + n_outer - 1, n_outer), i)

    barrier = pltpu.get_barrier_semaphore()
    for peer in (behind, below):
        pl.semaphore_signal(barrier, inc=1, device_id=peer, device_id_type=MESH)

    local = [
        pltpu.make_async_copy(exp_hbm, exp_ref, local_sem.at[0]),
        pltpu.make_async_copy(pos_hbm, pos_ref, local_sem.at[1]),
        pltpu.make_async_copy(kv_hbm.at[pl.ds(0, SPAN)], kvb.at[0], local_sem.at[2]),
        pltpu.make_async_copy(kv_hbm.at[pl.ds(SPAN, SPAN)], kvb.at[1], local_sem.at[3]),
        pltpu.make_async_copy(q_hbm, q_in, local_sem.at[4]),
    ]
    for part in local:
        part.start()

    def copy(src, dst, sent, arrived, device):
        return pltpu.make_async_remote_copy(
            src_ref=src, dst_ref=dst, send_sem=sent, recv_sem=arrived, device_id=device, device_id_type=MESH
        )

    def chunk_copy(src, chunk, device):
        return copy(src, kvb.at[chunk], send_sem.at[chunk], recv_sem.at[chunk], device)

    def note_copy(src, block, device):
        return copy(src, notes.at[block], note_send.at[block], note_recv.at[block], device)

    pl.semaphore_wait(barrier, 2)
    def send_own(s):
        rows = kv_hbm.at[pl.ds(s * SPAN, SPAN)]
        chunk_copy(rows, 4 + s, ahead).start()
        chunk_copy(rows, 2 + s, above).start()

    send_own(0)

    local[0].wait()
    local[1].wait()
    row = lax.broadcasted_iota(jnp.int32, (16, 128), 0)
    note = jnp.zeros((16, 128), F32)
    for side in range(2):
        for g in range(4):
            e = exp_ref[side, g]
            note = jnp.where(row == 4 * side + g, jnp.where(e > 0, 2.0, jnp.where(e < 0, 0.5, 1.0)), note)
    for s in range(2):
        index = lax.div(pos_ref[s * SPAN], SPAN)
        note = jnp.where(row == 8 + 2 * s, lax.div(index, 32).astype(F32), note)
        note = jnp.where(row == 9 + 2 * s, lax.rem(index, 32).astype(F32), note)
    notes[0] = note.astype(BF16)
    note_copy(notes.at[0], 2, ahead).start()
    note_copy(notes.at[0], 1, above).start()
    send_own(1)

    late = z < 3
    turns = {
        4: jnp.where(late, 4, 2),
        5: jnp.where(late, 5, 3),
        6: jnp.where(late, 6, 5),
        7: jnp.int32(7),
    }

    def arrive(chunk):
        chunk_copy(kvb.at[chunk], chunk, ahead).wait_recv()

    def exchange(t):
        for chunk, turn in turns.items():
            @pl.when(t == turn)
            def _(chunk=chunk):
                block = chunk // 2
                if chunk % 2 == 0:
                    note_copy(notes.at[block], block, ahead).wait_recv()
                    note_copy(notes.at[block], block + 1, ahead).start()
                arrive(chunk)
                chunk_copy(kvb.at[chunk], chunk + 2, ahead).start()

    local[4].wait()
    for h in range(HEADS):
        x = q_in[:, h * DIM : (h + 1) * DIM].astype(F32) * SCALE
        hi = x.astype(BF16)
        q2[h, :, 0:DIM] = hi
        q2[h, :, DIM : 2 * DIM] = (x - hi.astype(F32)).astype(BF16)
    mx[...] = jnp.full(mx.shape, -BIG, F32)
    acc[...] = jnp.zeros(acc.shape, F32)
    va[:, DIM : 2 * DIM] = jnp.ones((SPAN, DIM), BF16)

    def unpack(block, span):
        note = notes[block].astype(F32)

        def of(low, high):
            return jnp.where(span == 0, note[low : low + 1], note[high : high + 1])

        for g in range(2):
            rows = pl.ds(g * GROUP, GROUP)
            k = kvb[2 * block + span, rows, 0:DIM].astype(F32) * of(g, 2 + g)
            k = k.T.astype(BF16)
            kt[0:DIM, g * GROUP : (g + 1) * GROUP] = k
            kt[DIM : 2 * DIM, g * GROUP : (g + 1) * GROUP] = k
            v = kvb[2 * block + span, rows, DIM : 2 * DIM].astype(F32) * of(4 + g, 6 + g)
            va[rows, 0:DIM] = v.astype(BF16)
        return of(8, 10) * 32.0 + of(9, 11)

    def attend(h, penalty):
        s = jnp.dot(q2[h], kt[...], preferred_element_type=F32)
        if penalty is None:
            s = s + bias[...]
        m_old = mx[h]
        m_new, p = [], []
        for r in range(2):
            rows = slice(r * SPAN, (r + 1) * SPAN)
            a, b = s[rows, 0:128], s[rows, 128:256]
            top = jnp.max(jnp.maximum(a, b), axis=1, keepdims=True)
            if penalty is None:
                m = jnp.maximum(m_old[rows], top)
                off = m
            else:
                m = jnp.maximum(m_old[rows], top - penalty[r])
                off = m + penalty[r]
            m_new.append(m)
            p.append(jnp.concatenate([jnp.exp2(a - off), jnp.exp2(b - off)], axis=1).astype(BF16))
        m_new = jnp.concatenate(m_new, axis=0)
        alpha = jnp.exp2(m_old - m_new)
        add = jnp.dot(jnp.concatenate(p, axis=0), va[...], preferred_element_type=F32)
        numer = acc[h, :, 0:DIM] * alpha + add[:, 0:DIM]
        total = acc[h, :, DIM : 2 * DIM] * alpha + add[:, DIM : 2 * DIM]
        return m_new, numer, total

    def update(penalty):
        for h in range(HEADS):
            m_new, numer, total = attend(h, penalty)
            mx[h] = m_new
            acc[h, :, 0:DIM] = numer
            acc[h, :, DIM : 2 * DIM] = total

    note = notes[0].astype(F32)
    mine = [note[8 + 2 * r : 9 + 2 * r] * 32.0 + note[9 + 2 * r : 10 + 2 * r] for r in range(2)]

    def penalties(place):
        return [jnp.where(place < mine[r], 0.0, BIG) for r in range(2)]

    local[2].wait()
    local[3].wait()

    def own_step(s, carry):
        place = unpack(0, s)
        row = lax.broadcasted_iota(jnp.int32, (SPAN, 128), 0)
        col = lax.broadcasted_iota(jnp.int32, (SPAN, 128), 1)
        for r in range(2):
            apart = (mine[r] - place) * SPAN
            for c in range(2):
                beyond = (row - col - c * 128).astype(F32) + apart
                bias[r * SPAN : (r + 1) * SPAN, c * 128 : (c + 1) * 128] = jnp.where(beyond >= 0, 0.0, -BIG)
        update(None)
        return carry

    lax.fori_loop(0, 2, own_step, 0)

    def step(t, carry):
        exchange(t)

        @pl.when(jnp.logical_or(t == 2, t == 8))
        def _():
            block = t // 2
            note_copy(notes.at[block], block, ahead).wait_recv()

        @pl.when(jnp.logical_or(t < 4, t == 8))
        def _():
            arrive(t)

        update(penalties(unpack(t // 2, lax.rem(t, 2))))
        return carry

    lax.fori_loop(2, CHUNKS - 1, step, 0)

    arrive(CHUNKS - 1)
    penalty = penalties(unpack(BLOCKS - 1, 1))
    for h in range(HEADS):
        _, numer, total = attend(h, penalty)
        out_ref[:, h * DIM : (h + 1) * DIM] = (numer / total).astype(BF16)

    for chunk in range(2, CHUNKS):
        chunk_copy(kvb.at[chunk], chunk, ahead).wait_send()
    for block in range(1, BLOCKS):
        note_copy(notes.at[block], block, ahead).wait_send()


def solution(mesh):
    n_outer, n_inner = mesh.shape["outer"], mesh.shape["inner"]

    def local(queries, kv_codes, scale_exp, positions):
        tokens = queries.shape[0]
        in_hbm = pl.BlockSpec(memory_space=pltpu.HBM)
        operands = [queries, kv_codes, scale_exp.T, positions]
        return pl.pallas_call(
            functools.partial(kernel, n_outer, n_inner),
            out_shape=pltpu.VMEM((tokens, HEADS * DIM), BF16),
            in_specs=[in_hbm] * 4,
            out_specs=pl.BlockSpec(memory_space=pltpu.VMEM),
            scratch_shapes=[
                pltpu.SMEM((2, tokens // GROUP), jnp.int32),
                pltpu.SMEM((tokens,), jnp.int32),
                pltpu.VMEM((tokens, HEADS * DIM), BF16),
                pltpu.VMEM((CHUNKS, SPAN, 2 * DIM), BF16),
                pltpu.VMEM((BLOCKS, 16, 128), BF16),
                pltpu.VMEM((HEADS, tokens, 2 * DIM), BF16),
                pltpu.VMEM((2 * DIM, SPAN), BF16),
                pltpu.VMEM((SPAN, 2 * DIM), BF16),
                pltpu.VMEM((HEADS, tokens, 2 * DIM), F32),
                pltpu.VMEM((HEADS, tokens, 128), F32),
                pltpu.VMEM((tokens, SPAN), F32),
                pltpu.SemaphoreType.DMA((5,)),
                pltpu.SemaphoreType.DMA((CHUNKS,)),
                pltpu.SemaphoreType.DMA((CHUNKS,)),
                pltpu.SemaphoreType.DMA((BLOCKS,)),
                pltpu.SemaphoreType.DMA((BLOCKS,)),
            ],
            compiler_params=pltpu.CompilerParams(
                collective_id=0, has_side_effects=True, vmem_limit_bytes=40 * 2**20
            ),
            name="span_attention",
        )(*[pltpu.with_memory_space_constraint(x, pltpu.HBM) for x in operands])

    split = P(("outer", "inner"), None)
    return jax.shard_map(
        local,
        mesh=mesh,
        in_specs=(split, split, split, P(("outer", "inner"))),
        out_specs=split,
        check_vma=False,
    )
```

```python
import functools
import math

import jax
import jax.numpy as jnp
from jax import lax
from jax.experimental import pallas as pl
from jax.experimental.pallas import tpu as pltpu
from jax.sharding import PartitionSpec as P

MESH = pl.DeviceIdType.MESH
HEADS = 8
DIM = 128
SPAN = 256
GROUP = 128
BIG = 1e30
SCALE = math.log2(math.e) / math.sqrt(128.0)
BF16 = jnp.bfloat16
F32 = jnp.float32

BLOCKS, CHUNKS = 5, 10


def kernel(
    n_outer, n_inner,
    q_hbm, kv_hbm, exp_hbm, pos_hbm, out_ref,
    exp_ref, pos_ref, q_in, kvb, notes, q2, kt, va, acc, mx, bias, weights,
    local_sem, send_sem, recv_sem, note_send, note_recv,
):
    o, i = lax.axis_index("outer"), lax.axis_index("inner")
    z = lax.rem(i, 16)
    ahead = (o, lax.rem(i + 1, n_inner))
    behind = (o, lax.rem(i + n_inner - 1, n_inner))
    above = (lax.rem(o + 1, n_outer), i)
    below = (lax.rem(o + n_outer - 1, n_outer), i)

    barrier = pltpu.get_barrier_semaphore()
    for peer in (behind, below):
        pl.semaphore_signal(barrier, inc=1, device_id=peer, device_id_type=MESH)

    local = [
        pltpu.make_async_copy(exp_hbm, exp_ref, local_sem.at[0]),
        pltpu.make_async_copy(pos_hbm, pos_ref, local_sem.at[1]),
        pltpu.make_async_copy(kv_hbm.at[pl.ds(0, SPAN)], kvb.at[0], local_sem.at[2]),
        pltpu.make_async_copy(kv_hbm.at[pl.ds(SPAN, SPAN)], kvb.at[1], local_sem.at[3]),
        pltpu.make_async_copy(q_hbm, q_in, local_sem.at[4]),
    ]
    for part in local:
        part.start()

    def copy(src, dst, sent, arrived, device):
        return pltpu.make_async_remote_copy(
            src_ref=src, dst_ref=dst, send_sem=sent, recv_sem=arrived, device_id=device, device_id_type=MESH
        )

    def chunk_copy(src, chunk, device):
        return copy(src, kvb.at[chunk], send_sem.at[chunk], recv_sem.at[chunk], device)

    def half_copy(src, side, device):
        half = pl.ds(side * DIM, DIM)
        sem = CHUNKS - 1 + side
        return copy(src.at[:, half], kvb.at[CHUNKS - 1, :, half], send_sem.at[sem], recv_sem.at[sem], device)

    def note_copy(src, block, device):
        return copy(src, notes.at[block], note_send.at[block], note_recv.at[block], device)

    pl.semaphore_wait(barrier, 2)
    def send_own(s):
        rows = kv_hbm.at[pl.ds(s * SPAN, SPAN)]
        chunk_copy(rows, 4 + s, ahead).start()
        chunk_copy(rows, 2 + s, above).start()

    send_own(0)

    local[0].wait()
    local[1].wait()
    row = lax.broadcasted_iota(jnp.int32, (16, 128), 0)
    note = jnp.zeros((16, 128), F32)
    for side in range(2):
        for g in range(4):
            e = exp_ref[side, g]
            note = jnp.where(row == 4 * side + g, jnp.where(e > 0, 2.0, jnp.where(e < 0, 0.5, 1.0)), note)
    for s in range(2):
        index = lax.div(pos_ref[s * SPAN], SPAN)
        note = jnp.where(row == 8 + 2 * s, lax.div(index, 32).astype(F32), note)
        note = jnp.where(row == 9 + 2 * s, lax.rem(index, 32).astype(F32), note)
    notes[0] = note.astype(BF16)
    note_copy(notes.at[0], 2, ahead).start()
    note_copy(notes.at[0], 1, above).start()
    send_own(1)

    late = z < 3
    turns = {
        4: jnp.where(late, 4, 2),
        5: jnp.where(late, 5, 3),
        6: jnp.where(late, 6, 5),
        7: jnp.int32(7),
    }

    def arrive(chunk):
        chunk_copy(kvb.at[chunk], chunk, ahead).wait_recv()

    def exchange(t):
        for chunk, turn in turns.items():
            @pl.when(t == turn)
            def _(chunk=chunk):
                block = chunk // 2
                if chunk % 2 == 0:
                    note_copy(notes.at[block], block, ahead).wait_recv()
                    note_copy(notes.at[block], block + 1, ahead).start()
                arrive(chunk)
                if chunk + 2 < CHUNKS - 1:
                    chunk_copy(kvb.at[chunk], chunk + 2, ahead).start()
                else:
                    for side in range(2):
                        half_copy(kvb.at[chunk], side, ahead).start()

    local[4].wait()
    for h in range(HEADS):
        x = q_in[:, h * DIM : (h + 1) * DIM].astype(F32) * SCALE
        hi = x.astype(BF16)
        q2[h, :, 0:DIM] = hi
        q2[h, :, DIM : 2 * DIM] = (x - hi.astype(F32)).astype(BF16)
    mx[...] = jnp.full(mx.shape, -BIG, F32)
    acc[...] = jnp.zeros(acc.shape, F32)
    va[:, DIM : 2 * DIM] = jnp.ones((SPAN, DIM), BF16)

    def unpack(block, span, sides=(0, 1)):
        note = notes[block].astype(F32)

        def of(low, high):
            return jnp.where(span == 0, note[low : low + 1], note[high : high + 1])

        for g in range(2):
            rows = pl.ds(g * GROUP, GROUP)
            if 0 in sides:
                k = kvb[2 * block + span, rows, 0:DIM].astype(F32) * of(g, 2 + g)
                k = k.T.astype(BF16)
                kt[0:DIM, g * GROUP : (g + 1) * GROUP] = k
                kt[DIM : 2 * DIM, g * GROUP : (g + 1) * GROUP] = k
            if 1 in sides:
                v = kvb[2 * block + span, rows, DIM : 2 * DIM].astype(F32) * of(4 + g, 6 + g)
                va[rows, 0:DIM] = v.astype(BF16)
        return of(8, 10) * 32.0 + of(9, 11)

    def weigh(h, penalty):
        s = jnp.dot(q2[h], kt[...], preferred_element_type=F32)
        if penalty is None:
            s = s + bias[...]
        m_old = mx[h]
        m_new, p = [], []
        for r in range(2):
            rows = slice(r * SPAN, (r + 1) * SPAN)
            a, b = s[rows, 0:128], s[rows, 128:256]
            top = jnp.max(jnp.maximum(a, b), axis=1, keepdims=True)
            if penalty is None:
                m = jnp.maximum(m_old[rows], top)
                off = m
            else:
                m = jnp.maximum(m_old[rows], top - penalty[r])
                off = m + penalty[r]
            m_new.append(m)
            p.append(jnp.concatenate([jnp.exp2(a - off), jnp.exp2(b - off)], axis=1).astype(BF16))
        m_new = jnp.concatenate(m_new, axis=0)
        return m_new, jnp.exp2(m_old - m_new), jnp.concatenate(p, axis=0)

    def gather(h, alpha, p):
        add = jnp.dot(p, va[...], preferred_element_type=F32)
        numer = acc[h, :, 0:DIM] * alpha + add[:, 0:DIM]
        total = acc[h, :, DIM : 2 * DIM] * alpha + add[:, DIM : 2 * DIM]
        return numer, total

    def update(penalty):
        for h in range(HEADS):
            m_new, alpha, p = weigh(h, penalty)
            numer, total = gather(h, alpha, p)
            mx[h] = m_new
            acc[h, :, 0:DIM] = numer
            acc[h, :, DIM : 2 * DIM] = total

    note = notes[0].astype(F32)
    mine = [note[8 + 2 * r : 9 + 2 * r] * 32.0 + note[9 + 2 * r : 10 + 2 * r] for r in range(2)]

    def penalties(place):
        return [jnp.where(place < mine[r], 0.0, BIG) for r in range(2)]

    local[2].wait()
    local[3].wait()

    def own_step(s, carry):
        place = unpack(0, s)
        row = lax.broadcasted_iota(jnp.int32, (SPAN, 128), 0)
        col = lax.broadcasted_iota(jnp.int32, (SPAN, 128), 1)
        for r in range(2):
            apart = (mine[r] - place) * SPAN
            for c in range(2):
                beyond = (row - col - c * 128).astype(F32) + apart
                bias[r * SPAN : (r + 1) * SPAN, c * 128 : (c + 1) * 128] = jnp.where(beyond >= 0, 0.0, -BIG)
        update(None)
        return carry

    lax.fori_loop(0, 2, own_step, 0)

    def step(t, carry):
        exchange(t)

        @pl.when(jnp.logical_or(t == 2, t == 8))
        def _():
            block = t // 2
            note_copy(notes.at[block], block, ahead).wait_recv()

        @pl.when(jnp.logical_or(t < 4, t == 8))
        def _():
            arrive(t)

        update(penalties(unpack(t // 2, lax.rem(t, 2))))
        return carry

    lax.fori_loop(2, CHUNKS - 1, step, 0)

    half_copy(kvb.at[CHUNKS - 1], 0, ahead).wait_recv()
    penalty = penalties(unpack(BLOCKS - 1, 1, (0,)))
    for h in range(HEADS):
        _, alpha, p = weigh(h, penalty)
        mx[h] = alpha
        weights[h] = p
    half_copy(kvb.at[CHUNKS - 1], 1, ahead).wait_recv()
    unpack(BLOCKS - 1, 1, (1,))
    for h in range(HEADS):
        numer, total = gather(h, mx[h], weights[h])
        out_ref[:, h * DIM : (h + 1) * DIM] = (numer / total).astype(BF16)

    for chunk in range(2, CHUNKS - 1):
        chunk_copy(kvb.at[chunk], chunk, ahead).wait_send()
    for side in range(2):
        half_copy(kvb.at[CHUNKS - 1], side, ahead).wait_send()
    for block in range(1, BLOCKS):
        note_copy(notes.at[block], block, ahead).wait_send()


def solution(mesh):
    n_outer, n_inner = mesh.shape["outer"], mesh.shape["inner"]

    def local(queries, kv_codes, scale_exp, positions):
        tokens = queries.shape[0]
        in_hbm = pl.BlockSpec(memory_space=pltpu.HBM)
        operands = [queries, kv_codes, scale_exp.T, positions]
        return pl.pallas_call(
            functools.partial(kernel, n_outer, n_inner),
            out_shape=pltpu.VMEM((tokens, HEADS * DIM), BF16),
            in_specs=[in_hbm] * 4,
            out_specs=pl.BlockSpec(memory_space=pltpu.VMEM),
            scratch_shapes=[
                pltpu.SMEM((2, tokens // GROUP), jnp.int32),
                pltpu.SMEM((tokens,), jnp.int32),
                pltpu.VMEM((tokens, HEADS * DIM), BF16),
                pltpu.VMEM((CHUNKS, SPAN, 2 * DIM), BF16),
                pltpu.VMEM((BLOCKS, 16, 128), BF16),
                pltpu.VMEM((HEADS, tokens, 2 * DIM), BF16),
                pltpu.VMEM((2 * DIM, SPAN), BF16),
                pltpu.VMEM((SPAN, 2 * DIM), BF16),
                pltpu.VMEM((HEADS, tokens, 2 * DIM), F32),
                pltpu.VMEM((HEADS, tokens, 128), F32),
                pltpu.VMEM((tokens, SPAN), F32),
                pltpu.VMEM((HEADS, tokens, SPAN), BF16),
                pltpu.SemaphoreType.DMA((5,)),
                pltpu.SemaphoreType.DMA((CHUNKS + 1,)),
                pltpu.SemaphoreType.DMA((CHUNKS + 1,)),
                pltpu.SemaphoreType.DMA((BLOCKS,)),
                pltpu.SemaphoreType.DMA((BLOCKS,)),
            ],
            compiler_params=pltpu.CompilerParams(
                collective_id=0, has_side_effects=True, vmem_limit_bytes=40 * 2**20
            ),
            name="span_attention",
        )(*[pltpu.with_memory_space_constraint(x, pltpu.HBM) for x in operands])

    split = P(("outer", "inner"), None)
    return jax.shard_map(
        local,
        mesh=mesh,
        in_specs=(split, split, split, P(("outer", "inner"))),
        out_specs=split,
        check_vma=False,
    )
```

```python
import functools
import math

import jax
import jax.numpy as jnp
from jax import lax
from jax.experimental import pallas as pl
from jax.experimental.pallas import tpu as pltpu
from jax.sharding import PartitionSpec as P

MESH = pl.DeviceIdType.MESH
HEADS = 8
DIM = 128
SPAN = 256
GROUP = 128
BIG = 1e30
SCALE = math.log2(math.e) / math.sqrt(128.0)
BF16 = jnp.bfloat16
F32 = jnp.float32

BLOCKS, CHUNKS = 5, 10
LAST_Z, FAR_Z, MID_Z = 15, 13, 6
MID_TURN = 6
SIDES = (0, 1)


def gather(acc, va, h, alpha, p):
    add = jnp.dot(p, va[...], preferred_element_type=F32)
    numer = acc[h, :, 0:DIM] * alpha + add[:, 0:DIM]
    total = acc[h, :, DIM : 2 * DIM] * alpha + add[:, DIM : 2 * DIM]
    return numer, total


def finish(acc, alpha, weights, va, out_hbm, stage, sem):
    outs = []
    for h in range(HEADS):
        numer, total = gather(acc, va, h, alpha[h], weights[h])
        stage[h] = (numer / total).astype(BF16)
        outs.append(pltpu.make_async_copy(stage.at[h], out_hbm.at[:, pl.ds(h * DIM, DIM)], sem.at[h]))
        outs[h].start()
    for out in outs:
        out.wait()


def kernel(
    n_outer, n_inner,
    q_hbm, kv_hbm, exp_hbm, pos_hbm, acc, mx, weights, va,
    exp_ref, pos_ref, q_in, kvb, notes, relay, q2, kt, bias,
    local_sem, send_sem, recv_sem, note_send, note_recv, far_send, far_recv, mid_send,
):
    o, i = lax.axis_index("outer"), lax.axis_index("inner")
    z = lax.rem(i, 16)
    ahead = (o, lax.rem(i + 1, n_inner))
    behind = (o, lax.rem(i + n_inner - 1, n_inner))
    above = (lax.rem(o + 1, n_outer), i)
    below = (lax.rem(o + n_outer - 1, n_outer), i)

    barrier = pltpu.get_barrier_semaphore()
    for peer in (behind, below):
        pl.semaphore_signal(barrier, inc=1, device_id=peer, device_id_type=MESH)

    def at(i):
        return (o, lax.rem(i + n_inner, n_inner))

    core_1 = lax.rem(o, 2) == 1
    far, mid = jnp.logical_and(core_1, z == FAR_Z), jnp.logical_and(core_1, z == MID_Z)
    first, last = jnp.logical_and(core_1, z == 0), jnp.logical_and(core_1, z == LAST_Z)

    @pl.when(first)
    def _():
        pl.semaphore_signal(barrier, inc=1, device_id=at(i + MID_Z), device_id_type=MESH)

    @pl.when(mid)
    def _():
        peer = at(i + 16 + FAR_Z - MID_Z)
        pl.semaphore_signal(barrier, inc=1, device_id=peer, device_id_type=MESH)

    local = [
        pltpu.make_async_copy(exp_hbm, exp_ref, local_sem.at[0]),
        pltpu.make_async_copy(pos_hbm, pos_ref, local_sem.at[1]),
        pltpu.make_async_copy(kv_hbm.at[pl.ds(0, SPAN)], kvb.at[0], local_sem.at[2]),
        pltpu.make_async_copy(kv_hbm.at[pl.ds(SPAN, SPAN)], kvb.at[1], local_sem.at[3]),
        pltpu.make_async_copy(q_hbm, q_in, local_sem.at[4]),
    ]
    for part in local:
        part.start()

    def copy(src, dst, sent, arrived, device):
        return pltpu.make_async_remote_copy(
            src_ref=src, dst_ref=dst, send_sem=sent, recv_sem=arrived, device_id=device, device_id_type=MESH
        )

    def chunk_copy(src, chunk, device):
        return copy(src, kvb.at[chunk], send_sem.at[chunk], recv_sem.at[chunk], device)

    def half_copy(src, side, device):
        half = pl.ds(side * DIM, DIM)
        sem = CHUNKS - 1 + side
        return copy(src.at[:, half], kvb.at[CHUNKS - 1, :, half], send_sem.at[sem], recv_sem.at[sem], device)

    def note_copy(src, block, device):
        return copy(src, notes.at[block], note_send.at[block], note_recv.at[block], device)

    def to_relay(side, device):
        src = kv_hbm.at[pl.ds(SPAN, SPAN), pl.ds(side * DIM, DIM)]
        return copy(src, relay.at[side], far_send.at[side], far_recv.at[side], device)

    def from_relay(side, device):
        dst = kvb.at[CHUNKS - 1, :, pl.ds(side * DIM, DIM)]
        return copy(relay.at[side], dst, mid_send.at[side], recv_sem.at[CHUNKS - 1 + side], device)

    relays = jnp.logical_or(far, mid)

    @pl.when(relays)
    def _():
        pl.semaphore_wait(barrier, 3)

    @pl.when(jnp.logical_not(relays))
    def _():
        pl.semaphore_wait(barrier, 2)

    @pl.when(far)
    def _():
        for side in SIDES:
            to_relay(side, at(i + 16 - FAR_Z + MID_Z)).start()

    def send_own(s):
        rows = kv_hbm.at[pl.ds(s * SPAN, SPAN)]
        chunk_copy(rows, 4 + s, ahead).start()
        chunk_copy(rows, 2 + s, above).start()

    send_own(0)

    local[0].wait()
    local[1].wait()
    row = lax.broadcasted_iota(jnp.int32, (16, 128), 0)
    note = jnp.zeros((16, 128), F32)
    for side in range(2):
        for g in range(4):
            e = exp_ref[side, g]
            note = jnp.where(row == 4 * side + g, jnp.where(e > 0, 2.0, jnp.where(e < 0, 0.5, 1.0)), note)
    for s in range(2):
        index = lax.div(pos_ref[s * SPAN], SPAN)
        note = jnp.where(row == 8 + 2 * s, lax.div(index, 32).astype(F32), note)
        note = jnp.where(row == 9 + 2 * s, lax.rem(index, 32).astype(F32), note)
    notes[0] = note.astype(BF16)
    note_copy(notes.at[0], 2, ahead).start()
    note_copy(notes.at[0], 1, above).start()
    send_own(1)

    late = z < 3
    turns = {
        4: jnp.where(late, 4, 2),
        5: jnp.where(late, 5, 3),
        6: jnp.where(late, 6, 5),
        7: jnp.where(z > 10, 6, 7),
    }

    def arrive(chunk):
        chunk_copy(kvb.at[chunk], chunk, ahead).wait_recv()

    def exchange(t):
        @pl.when(jnp.logical_and(mid, t == MID_TURN))
        def _():
            for side in SIDES:
                to_relay(side, ahead).wait_recv()
                from_relay(side, at(i - MID_Z)).start()

        for chunk, turn in turns.items():
            @pl.when(t == turn)
            def _(chunk=chunk):
                block = chunk // 2
                if chunk % 2 == 0:
                    note_copy(notes.at[block], block, ahead).wait_recv()
                    note_copy(notes.at[block], block + 1, ahead).start()
                arrive(chunk)
                if chunk + 2 < CHUNKS - 1:
                    chunk_copy(kvb.at[chunk], chunk + 2, ahead).start()
                else:
                    for side in range(2):
                        @pl.when(jnp.logical_not(last) if side in SIDES else z >= 0)
                        def _(side=side):
                            half_copy(kvb.at[chunk], side, ahead).start()

    local[4].wait()
    for h in range(HEADS):
        x = q_in[:, h * DIM : (h + 1) * DIM].astype(F32) * SCALE
        hi = x.astype(BF16)
        q2[h, :, 0:DIM] = hi
        q2[h, :, DIM : 2 * DIM] = (x - hi.astype(F32)).astype(BF16)
    mx[...] = jnp.full(mx.shape, -BIG, F32)
    acc[...] = jnp.zeros(acc.shape, F32)
    va[:, DIM : 2 * DIM] = jnp.ones((SPAN, DIM), BF16)

    def unpack(block, span, sides=(0, 1)):
        note = notes[block].astype(F32)

        def of(low, high):
            return jnp.where(span == 0, note[low : low + 1], note[high : high + 1])

        for g in range(2):
            rows = pl.ds(g * GROUP, GROUP)
            if 0 in sides:
                k = kvb[2 * block + span, rows, 0:DIM].astype(F32) * of(g, 2 + g)
                k = k.T.astype(BF16)
                kt[0:DIM, g * GROUP : (g + 1) * GROUP] = k
                kt[DIM : 2 * DIM, g * GROUP : (g + 1) * GROUP] = k
            if 1 in sides:
                v = kvb[2 * block + span, rows, DIM : 2 * DIM].astype(F32) * of(4 + g, 6 + g)
                va[rows, 0:DIM] = v.astype(BF16)
        return of(8, 10) * 32.0 + of(9, 11)

    def weigh(h, penalty):
        s = jnp.dot(q2[h], kt[...], preferred_element_type=F32)
        if penalty is None:
            s = s + bias[...]
        m_old = mx[h]
        m_new, p = [], []
        for r in range(2):
            rows = slice(r * SPAN, (r + 1) * SPAN)
            a, b = s[rows, 0:128], s[rows, 128:256]
            top = jnp.max(jnp.maximum(a, b), axis=1, keepdims=True)
            if penalty is None:
                m = jnp.maximum(m_old[rows], top)
                off = m
            else:
                m = jnp.maximum(m_old[rows], top - penalty[r])
                off = m + penalty[r]
            m_new.append(m)
            p.append(jnp.concatenate([jnp.exp2(a - off), jnp.exp2(b - off)], axis=1).astype(BF16))
        m_new = jnp.concatenate(m_new, axis=0)
        return m_new, jnp.exp2(m_old - m_new), jnp.concatenate(p, axis=0)

    def update(penalty):
        for h in range(HEADS):
            m_new, alpha, p = weigh(h, penalty)
            numer, total = gather(acc, va, h, alpha, p)
            mx[h] = m_new
            acc[h, :, 0:DIM] = numer
            acc[h, :, DIM : 2 * DIM] = total

    note = notes[0].astype(F32)
    mine = [note[8 + 2 * r : 9 + 2 * r] * 32.0 + note[9 + 2 * r : 10 + 2 * r] for r in range(2)]

    def penalties(place):
        return [jnp.where(place < mine[r], 0.0, BIG) for r in range(2)]

    local[2].wait()
    local[3].wait()

    def own_step(s, carry):
        place = unpack(0, s)
        row = lax.broadcasted_iota(jnp.int32, (SPAN, 128), 0)
        col = lax.broadcasted_iota(jnp.int32, (SPAN, 128), 1)
        for r in range(2):
            apart = (mine[r] - place) * SPAN
            for c in range(2):
                beyond = (row - col - c * 128).astype(F32) + apart
                bias[r * SPAN : (r + 1) * SPAN, c * 128 : (c + 1) * 128] = jnp.where(beyond >= 0, 0.0, -BIG)
        update(None)
        return carry

    lax.fori_loop(0, 2, own_step, 0)

    def step(t, carry):
        exchange(t)

        @pl.when(jnp.logical_or(t == 2, t == 8))
        def _():
            block = t // 2
            note_copy(notes.at[block], block, ahead).wait_recv()

        @pl.when(jnp.logical_or(t < 4, t == 8))
        def _():
            arrive(t)

        update(penalties(unpack(t // 2, lax.rem(t, 2))))
        return carry

    lax.fori_loop(2, CHUNKS - 1, step, 0)

    half_copy(kvb.at[CHUNKS - 1], 0, ahead).wait_recv()
    penalty = penalties(unpack(BLOCKS - 1, 1, (0,)))
    for h in range(HEADS):
        _, alpha, p = weigh(h, penalty)
        mx[h] = alpha
        weights[h] = p
    half_copy(kvb.at[CHUNKS - 1], 1, ahead).wait_recv()
    unpack(BLOCKS - 1, 1, (1,))

    for chunk in range(2, CHUNKS - 1):
        chunk_copy(kvb.at[chunk], chunk, ahead).wait_send()
    for side in range(2):
        @pl.when(jnp.logical_not(last) if side in SIDES else z >= 0)
        def _(side=side):
            half_copy(kvb.at[CHUNKS - 1], side, ahead).wait_send()

    @pl.when(far)
    def _():
        for side in SIDES:
            to_relay(side, ahead).wait_send()

    @pl.when(mid)
    def _():
        for side in SIDES:
            from_relay(side, ahead).wait_send()

    for block in range(1, BLOCKS):
        note_copy(notes.at[block], block, ahead).wait_send()


def solution(mesh):
    n_outer, n_inner = mesh.shape["outer"], mesh.shape["inner"]

    def local(queries, kv_codes, scale_exp, positions):
        tokens = queries.shape[0]
        in_hbm = pl.BlockSpec(memory_space=pltpu.HBM)
        operands = [queries, kv_codes, scale_exp.T, positions]
        in_vmem = pl.BlockSpec(memory_space=pltpu.VMEM)
        state = pl.pallas_call(
            functools.partial(kernel, n_outer, n_inner),
            out_shape=[
                pltpu.VMEM((HEADS, tokens, 2 * DIM), F32),
                pltpu.VMEM((HEADS, tokens, 128), F32),
                pltpu.VMEM((HEADS, tokens, SPAN), BF16),
                pltpu.VMEM((SPAN, 2 * DIM), BF16),
            ],
            in_specs=[in_hbm] * 4,
            out_specs=[in_vmem] * 4,
            scratch_shapes=[
                pltpu.SMEM((2, tokens // GROUP), jnp.int32),
                pltpu.SMEM((tokens,), jnp.int32),
                pltpu.VMEM((tokens, HEADS * DIM), BF16),
                pltpu.VMEM((CHUNKS, SPAN, 2 * DIM), BF16),
                pltpu.VMEM((BLOCKS, 16, 128), BF16),
                pltpu.VMEM((2, SPAN, DIM), BF16),
                pltpu.VMEM((HEADS, tokens, 2 * DIM), BF16),
                pltpu.VMEM((2 * DIM, SPAN), BF16),
                pltpu.VMEM((tokens, SPAN), F32),
                pltpu.SemaphoreType.DMA((5,)),
                pltpu.SemaphoreType.DMA((CHUNKS + 1,)),
                pltpu.SemaphoreType.DMA((CHUNKS + 1,)),
                pltpu.SemaphoreType.DMA((BLOCKS,)),
                pltpu.SemaphoreType.DMA((BLOCKS,)),
                pltpu.SemaphoreType.DMA((2,)),
                pltpu.SemaphoreType.DMA((2,)),
                pltpu.SemaphoreType.DMA((2,)),
            ],
            compiler_params=pltpu.CompilerParams(
                collective_id=0, has_side_effects=True, vmem_limit_bytes=32 * 2**20
            ),
            name="span_attention",
        )(*[pltpu.with_memory_space_constraint(x, pltpu.HBM) for x in operands])
        return pl.pallas_call(
            finish,
            out_shape=pltpu.HBM((tokens, HEADS * DIM), BF16),
            in_specs=[in_vmem] * 4,
            out_specs=in_hbm,
            scratch_shapes=[
                pltpu.VMEM((HEADS, tokens, DIM), BF16),
                pltpu.SemaphoreType.DMA((HEADS,)),
            ],
            compiler_params=pltpu.CompilerParams(vmem_limit_bytes=24 * 2**20),
            name="last_values",
        )(*state)

    split = P(("outer", "inner"), None)
    return jax.shard_map(
        local,
        mesh=mesh,
        in_specs=(split, split, split, P(("outer", "inner"))),
        out_specs=split,
        check_vma=False,
    )
```

```python
import functools
import math

import jax
import jax.numpy as jnp
from jax import lax
from jax.experimental import pallas as pl
from jax.experimental.pallas import tpu as pltpu
from jax.sharding import PartitionSpec as P

MESH = pl.DeviceIdType.MESH
HEADS = 8
DIM = 128
SPAN = 256
GROUP = 128
BIG = 1e30
SCALE = math.log2(math.e) / math.sqrt(128.0)
BF16 = jnp.bfloat16
F32 = jnp.float32

BLOCKS, CHUNKS = 5, 10
LAST_Z, FAR_Z, MID_Z = 15, 13, 6
PIECES, MID_TURNS = (2, 0, 1), {2: 6, 0: 7, 1: 7}


def gather(acc, va, h, alpha, p):
    add = jnp.dot(p, va[...], preferred_element_type=F32)
    numer = acc[h, :, 0:DIM] * alpha + add[:, 0:DIM]
    total = acc[h, :, DIM : 2 * DIM] * alpha + add[:, DIM : 2 * DIM]
    return numer, total


def finish(acc, alpha, weights, va, out_hbm, stage, sem):
    outs = []
    for h in range(HEADS):
        numer, total = gather(acc, va, h, alpha[h], weights[h])
        stage[h] = (numer / total).astype(BF16)
        outs.append(pltpu.make_async_copy(stage.at[h], out_hbm.at[:, pl.ds(h * DIM, DIM)], sem.at[h]))
        outs[h].start()
    for out in outs:
        out.wait()


def kernel(
    n_outer, n_inner,
    q_hbm, kv_hbm, exp_hbm, pos_hbm, acc, mx, weights, va,
    exp_ref, pos_ref, q_in, kvb, notes, relay, q2, kt, bias,
    local_sem, send_sem, recv_sem, note_send, note_recv, far_send, far_recv, mid_send,
):
    o, i = lax.axis_index("outer"), lax.axis_index("inner")
    z = lax.rem(i, 16)
    ahead = (o, lax.rem(i + 1, n_inner))
    behind = (o, lax.rem(i + n_inner - 1, n_inner))
    above = (lax.rem(o + 1, n_outer), i)
    below = (lax.rem(o + n_outer - 1, n_outer), i)

    barrier = pltpu.get_barrier_semaphore()
    for peer in (behind, below):
        pl.semaphore_signal(barrier, inc=1, device_id=peer, device_id_type=MESH)

    def at(i):
        return (o, lax.rem(i + n_inner, n_inner))

    core_1 = lax.rem(o, 2) == 1
    far, mid = jnp.logical_and(core_1, z == FAR_Z), jnp.logical_and(core_1, z == MID_Z)
    first, last = jnp.logical_and(core_1, z == 0), jnp.logical_and(core_1, z == LAST_Z)

    @pl.when(first)
    def _():
        pl.semaphore_signal(barrier, inc=1, device_id=at(i + MID_Z), device_id_type=MESH)

    @pl.when(mid)
    def _():
        peer = at(i + 16 + FAR_Z - MID_Z)
        pl.semaphore_signal(barrier, inc=1, device_id=peer, device_id_type=MESH)

    local = [
        pltpu.make_async_copy(exp_hbm, exp_ref, local_sem.at[0]),
        pltpu.make_async_copy(pos_hbm, pos_ref, local_sem.at[1]),
        pltpu.make_async_copy(kv_hbm.at[pl.ds(0, SPAN)], kvb.at[0], local_sem.at[2]),
        pltpu.make_async_copy(kv_hbm.at[pl.ds(SPAN, SPAN)], kvb.at[1], local_sem.at[3]),
        pltpu.make_async_copy(q_hbm, q_in, local_sem.at[4]),
    ]
    for part in local:
        part.start()

    def copy(src, dst, sent, arrived, device):
        return pltpu.make_async_remote_copy(
            src_ref=src, dst_ref=dst, send_sem=sent, recv_sem=arrived, device_id=device, device_id_type=MESH
        )

    def chunk_copy(src, chunk, device):
        return copy(src, kvb.at[chunk], send_sem.at[chunk], recv_sem.at[chunk], device)

    def half_copy(src, side, device):
        half = pl.ds(side * DIM, DIM)
        sem = CHUNKS - 1 + side
        return copy(src.at[:, half], kvb.at[CHUNKS - 1, :, half], send_sem.at[sem], recv_sem.at[sem], device)

    def note_copy(src, block, device):
        return copy(src, notes.at[block], note_send.at[block], note_recv.at[block], device)

    def lanes(piece):
        return pl.ds(0, 2 * DIM) if piece == 2 else pl.ds(piece * DIM, DIM)

    def to_relay(piece, device):
        src = kv_hbm.at[pl.ds(0 if piece == 2 else SPAN, SPAN), lanes(piece)]
        dst = relay.at[1 if piece == 2 else 0, :, lanes(piece)]
        return copy(src, dst, far_send.at[piece], far_recv.at[piece], device)

    def from_relay(piece, device):
        src = relay.at[1 if piece == 2 else 0, :, lanes(piece)]
        chunk, sem = (CHUNKS - 2, CHUNKS - 2) if piece == 2 else (CHUNKS - 1, CHUNKS - 1 + piece)
        return copy(src, kvb.at[chunk, :, lanes(piece)], mid_send.at[piece], recv_sem.at[sem], device)

    relays = jnp.logical_or(far, mid)

    @pl.when(relays)
    def _():
        pl.semaphore_wait(barrier, 3)

    @pl.when(jnp.logical_not(relays))
    def _():
        pl.semaphore_wait(barrier, 2)

    @pl.when(far)
    def _():
        for piece in PIECES:
            to_relay(piece, at(i + 16 - FAR_Z + MID_Z)).start()

    def send_own(s):
        rows = kv_hbm.at[pl.ds(s * SPAN, SPAN)]
        chunk_copy(rows, 4 + s, ahead).start()
        chunk_copy(rows, 2 + s, above).start()

    send_own(0)

    local[0].wait()
    local[1].wait()
    row = lax.broadcasted_iota(jnp.int32, (16, 128), 0)
    note = jnp.zeros((16, 128), F32)
    for side in range(2):
        for g in range(4):
            e = exp_ref[side, g]
            note = jnp.where(row == 4 * side + g, jnp.where(e > 0, 2.0, jnp.where(e < 0, 0.5, 1.0)), note)
    for s in range(2):
        index = lax.div(pos_ref[s * SPAN], SPAN)
        note = jnp.where(row == 8 + 2 * s, lax.div(index, 32).astype(F32), note)
        note = jnp.where(row == 9 + 2 * s, lax.rem(index, 32).astype(F32), note)
    notes[0] = note.astype(BF16)
    note_copy(notes.at[0], 2, ahead).start()
    note_copy(notes.at[0], 1, above).start()
    send_own(1)

    late = z < 3
    turns = {
        4: jnp.where(late, 4, 2),
        5: jnp.where(late, 5, 3),
        6: jnp.where(late, 6, 5),
        7: jnp.where(z > 10, 6, 7),
    }

    def arrive(chunk):
        chunk_copy(kvb.at[chunk], chunk, ahead).wait_recv()

    def exchange(t):
        for piece in PIECES:
            @pl.when(jnp.logical_and(mid, t == MID_TURNS[piece]))
            def _(piece=piece):
                to_relay(piece, ahead).wait_recv()
                from_relay(piece, at(i - MID_Z)).start()

        for chunk, turn in turns.items():
            @pl.when(t == turn)
            def _(chunk=chunk):
                block = chunk // 2
                if chunk % 2 == 0:
                    note_copy(notes.at[block], block, ahead).wait_recv()
                    note_copy(notes.at[block], block + 1, ahead).start()
                arrive(chunk)
                if chunk < 6:
                    chunk_copy(kvb.at[chunk], chunk + 2, ahead).start()
                else:
                    @pl.when(jnp.logical_not(last))
                    def _():
                        if chunk == 6:
                            chunk_copy(kvb.at[chunk], chunk + 2, ahead).start()
                        else:
                            for side in range(2):
                                half_copy(kvb.at[chunk], side, ahead).start()

    local[4].wait()
    for h in range(HEADS):
        x = q_in[:, h * DIM : (h + 1) * DIM].astype(F32) * SCALE
        hi = x.astype(BF16)
        q2[h, :, 0:DIM] = hi
        q2[h, :, DIM : 2 * DIM] = (x - hi.astype(F32)).astype(BF16)
    mx[...] = jnp.full(mx.shape, -BIG, F32)
    acc[...] = jnp.zeros(acc.shape, F32)
    va[:, DIM : 2 * DIM] = jnp.ones((SPAN, DIM), BF16)

    def unpack(block, span, sides=(0, 1)):
        note = notes[block].astype(F32)

        def of(low, high):
            return jnp.where(span == 0, note[low : low + 1], note[high : high + 1])

        for g in range(2):
            rows = pl.ds(g * GROUP, GROUP)
            if 0 in sides:
                k = kvb[2 * block + span, rows, 0:DIM].astype(F32) * of(g, 2 + g)
                k = k.T.astype(BF16)
                kt[0:DIM, g * GROUP : (g + 1) * GROUP] = k
                kt[DIM : 2 * DIM, g * GROUP : (g + 1) * GROUP] = k
            if 1 in sides:
                v = kvb[2 * block + span, rows, DIM : 2 * DIM].astype(F32) * of(4 + g, 6 + g)
                va[rows, 0:DIM] = v.astype(BF16)
        return of(8, 10) * 32.0 + of(9, 11)

    def weigh(h, penalty):
        s = jnp.dot(q2[h], kt[...], preferred_element_type=F32)
        if penalty is None:
            s = s + bias[...]
        m_old = mx[h]
        m_new, p = [], []
        for r in range(2):
            rows = slice(r * SPAN, (r + 1) * SPAN)
            a, b = s[rows, 0:128], s[rows, 128:256]
            top = jnp.max(jnp.maximum(a, b), axis=1, keepdims=True)
            if penalty is None:
                m = jnp.maximum(m_old[rows], top)
                off = m
            else:
                m = jnp.maximum(m_old[rows], top - penalty[r])
                off = m + penalty[r]
            m_new.append(m)
            p.append(jnp.concatenate([jnp.exp2(a - off), jnp.exp2(b - off)], axis=1).astype(BF16))
        m_new = jnp.concatenate(m_new, axis=0)
        return m_new, jnp.exp2(m_old - m_new), jnp.concatenate(p, axis=0)

    def update(penalty):
        for h in range(HEADS):
            m_new, alpha, p = weigh(h, penalty)
            numer, total = gather(acc, va, h, alpha, p)
            mx[h] = m_new
            acc[h, :, 0:DIM] = numer
            acc[h, :, DIM : 2 * DIM] = total

    note = notes[0].astype(F32)
    mine = [note[8 + 2 * r : 9 + 2 * r] * 32.0 + note[9 + 2 * r : 10 + 2 * r] for r in range(2)]

    def penalties(place):
        return [jnp.where(place < mine[r], 0.0, BIG) for r in range(2)]

    local[2].wait()
    local[3].wait()

    def own_step(s, carry):
        place = unpack(0, s)
        row = lax.broadcasted_iota(jnp.int32, (SPAN, 128), 0)
        col = lax.broadcasted_iota(jnp.int32, (SPAN, 128), 1)
        for r in range(2):
            apart = (mine[r] - place) * SPAN
            for c in range(2):
                beyond = (row - col - c * 128).astype(F32) + apart
                bias[r * SPAN : (r + 1) * SPAN, c * 128 : (c + 1) * 128] = jnp.where(beyond >= 0, 0.0, -BIG)
        update(None)
        return carry

    lax.fori_loop(0, 2, own_step, 0)

    def step(t, carry):
        exchange(t)

        @pl.when(jnp.logical_or(t == 2, t == 8))
        def _():
            block = t // 2
            note_copy(notes.at[block], block, ahead).wait_recv()

        @pl.when(jnp.logical_or(t < 4, t == 8))
        def _():
            arrive(t)

        update(penalties(unpack(t // 2, lax.rem(t, 2))))
        return carry

    lax.fori_loop(2, CHUNKS - 1, step, 0)

    half_copy(kvb.at[CHUNKS - 1], 0, ahead).wait_recv()
    penalty = penalties(unpack(BLOCKS - 1, 1, (0,)))
    for h in range(HEADS):
        _, alpha, p = weigh(h, penalty)
        mx[h] = alpha
        weights[h] = p
    half_copy(kvb.at[CHUNKS - 1], 1, ahead).wait_recv()
    unpack(BLOCKS - 1, 1, (1,))

    for chunk in range(2, CHUNKS - 2):
        chunk_copy(kvb.at[chunk], chunk, ahead).wait_send()

    @pl.when(jnp.logical_not(last))
    def _():
        chunk_copy(kvb.at[CHUNKS - 2], CHUNKS - 2, ahead).wait_send()
        for side in range(2):
            half_copy(kvb.at[CHUNKS - 1], side, ahead).wait_send()

    @pl.when(far)
    def _():
        for piece in PIECES:
            to_relay(piece, ahead).wait_send()

    @pl.when(mid)
    def _():
        for piece in PIECES:
            from_relay(piece, ahead).wait_send()

    for block in range(1, BLOCKS):
        note_copy(notes.at[block], block, ahead).wait_send()


def solution(mesh):
    n_outer, n_inner = mesh.shape["outer"], mesh.shape["inner"]

    def local(queries, kv_codes, scale_exp, positions):
        tokens = queries.shape[0]
        in_hbm = pl.BlockSpec(memory_space=pltpu.HBM)
        operands = [queries, kv_codes, scale_exp.T, positions]
        in_vmem = pl.BlockSpec(memory_space=pltpu.VMEM)
        state = pl.pallas_call(
            functools.partial(kernel, n_outer, n_inner),
            out_shape=[
                pltpu.VMEM((HEADS, tokens, 2 * DIM), F32),
                pltpu.VMEM((HEADS, tokens, 128), F32),
                pltpu.VMEM((HEADS, tokens, SPAN), BF16),
                pltpu.VMEM((SPAN, 2 * DIM), BF16),
            ],
            in_specs=[in_hbm] * 4,
            out_specs=[in_vmem] * 4,
            scratch_shapes=[
                pltpu.SMEM((2, tokens // GROUP), jnp.int32),
                pltpu.SMEM((tokens,), jnp.int32),
                pltpu.VMEM((tokens, HEADS * DIM), BF16),
                pltpu.VMEM((CHUNKS, SPAN, 2 * DIM), BF16),
                pltpu.VMEM((BLOCKS, 16, 128), BF16),
                pltpu.VMEM((2, SPAN, 2 * DIM), BF16),
                pltpu.VMEM((HEADS, tokens, 2 * DIM), BF16),
                pltpu.VMEM((2 * DIM, SPAN), BF16),
                pltpu.VMEM((tokens, SPAN), F32),
                pltpu.SemaphoreType.DMA((5,)),
                pltpu.SemaphoreType.DMA((CHUNKS + 1,)),
                pltpu.SemaphoreType.DMA((CHUNKS + 1,)),
                pltpu.SemaphoreType.DMA((BLOCKS,)),
                pltpu.SemaphoreType.DMA((BLOCKS,)),
                pltpu.SemaphoreType.DMA((3,)),
                pltpu.SemaphoreType.DMA((3,)),
                pltpu.SemaphoreType.DMA((3,)),
            ],
            compiler_params=pltpu.CompilerParams(
                collective_id=0, has_side_effects=True, vmem_limit_bytes=32 * 2**20
            ),
            name="span_attention",
        )(*[pltpu.with_memory_space_constraint(x, pltpu.HBM) for x in operands])
        return pl.pallas_call(
            finish,
            out_shape=pltpu.HBM((tokens, HEADS * DIM), BF16),
            in_specs=[in_vmem] * 4,
            out_specs=in_hbm,
            scratch_shapes=[
                pltpu.VMEM((HEADS, tokens, DIM), BF16),
                pltpu.SemaphoreType.DMA((HEADS,)),
            ],
            compiler_params=pltpu.CompilerParams(vmem_limit_bytes=24 * 2**20),
            name="last_values",
        )(*state)

    split = P(("outer", "inner"), None)
    return jax.shard_map(
        local,
        mesh=mesh,
        in_specs=(split, split, split, P(("outer", "inner"))),
        out_specs=split,
        check_vma=False,
    )
```

```python
import functools
import math

import jax
import jax.numpy as jnp
from jax import lax
from jax.experimental import pallas as pl
from jax.experimental.pallas import tpu as pltpu
from jax.sharding import PartitionSpec as P

MESH = pl.DeviceIdType.MESH
HEADS = 8
DIM = 128
SPAN = 256
GROUP = 128
BIG = 1e30
SCALE = math.log2(math.e) / math.sqrt(128.0)
BF16 = jnp.bfloat16
F32 = jnp.float32

BLOCKS, CHUNKS = 5, 10
LAST_Z, FAR_Z, MID_Z = 15, 13, 6
PIECES, MID_TURNS = (2, 0, 1), {2: 5, 0: 6, 1: 6}


def gather(acc, va, h, alpha, p):
    add = jnp.dot(p, va[...], preferred_element_type=F32)
    numer = acc[h, :, 0:DIM] * alpha + add[:, 0:DIM]
    total = acc[h, :, DIM : 2 * DIM] * alpha + add[:, DIM : 2 * DIM]
    return numer, total


def finish(acc, alpha, weights, va, out_hbm, stage, sem):
    outs = []
    for h in range(HEADS):
        numer, total = gather(acc, va, h, alpha[h], weights[h])
        stage[h] = (numer / total).astype(BF16)
        outs.append(pltpu.make_async_copy(stage.at[h], out_hbm.at[:, pl.ds(h * DIM, DIM)], sem.at[h]))
        outs[h].start()
    for out in outs:
        out.wait()


def kernel(
    n_outer, n_inner,
    q_hbm, kv_hbm, exp_hbm, pos_hbm, acc, mx, weights, va,
    exp_ref, pos_ref, q_in, kvb, notes, relay, q2, kt, bias,
    local_sem, send_sem, recv_sem, note_send, note_recv, far_send, far_recv, mid_send,
):
    o, i = lax.axis_index("outer"), lax.axis_index("inner")
    z = lax.rem(i, 16)
    ahead = (o, lax.rem(i + 1, n_inner))
    behind = (o, lax.rem(i + n_inner - 1, n_inner))
    above = (lax.rem(o + 1, n_outer), i)
    below = (lax.rem(o + n_outer - 1, n_outer), i)

    barrier = pltpu.get_barrier_semaphore()
    for peer in (behind, below):
        pl.semaphore_signal(barrier, inc=1, device_id=peer, device_id_type=MESH)

    def at(i):
        return (o, lax.rem(i + n_inner, n_inner))

    core_1 = lax.rem(o, 2) == 1
    far, mid = jnp.logical_and(core_1, z == FAR_Z), jnp.logical_and(core_1, z == MID_Z)
    first, last = jnp.logical_and(core_1, z == 0), jnp.logical_and(core_1, z == LAST_Z)

    @pl.when(first)
    def _():
        pl.semaphore_signal(barrier, inc=1, device_id=at(i + MID_Z), device_id_type=MESH)

    @pl.when(mid)
    def _():
        peer = at(i + 16 + FAR_Z - MID_Z)
        pl.semaphore_signal(barrier, inc=1, device_id=peer, device_id_type=MESH)

    local = [
        pltpu.make_async_copy(exp_hbm, exp_ref, local_sem.at[0]),
        pltpu.make_async_copy(pos_hbm, pos_ref, local_sem.at[1]),
        pltpu.make_async_copy(kv_hbm.at[pl.ds(0, SPAN)], kvb.at[0], local_sem.at[2]),
        pltpu.make_async_copy(kv_hbm.at[pl.ds(SPAN, SPAN)], kvb.at[1], local_sem.at[3]),
        pltpu.make_async_copy(q_hbm, q_in, local_sem.at[4]),
    ]
    for part in local:
        part.start()

    def copy(src, dst, sent, arrived, device):
        return pltpu.make_async_remote_copy(
            src_ref=src, dst_ref=dst, send_sem=sent, recv_sem=arrived, device_id=device, device_id_type=MESH
        )

    def chunk_copy(src, chunk, device):
        return copy(src, kvb.at[chunk], send_sem.at[chunk], recv_sem.at[chunk], device)

    def half_copy(src, side, device):
        half = pl.ds(side * DIM, DIM)
        sem = CHUNKS - 1 + side
        return copy(src.at[:, half], kvb.at[CHUNKS - 1, :, half], send_sem.at[sem], recv_sem.at[sem], device)

    def note_copy(src, block, device):
        return copy(src, notes.at[block], note_send.at[block], note_recv.at[block], device)

    def lanes(piece):
        return pl.ds(0, 2 * DIM) if piece == 2 else pl.ds(piece * DIM, DIM)

    def to_relay(piece, device):
        src = kv_hbm.at[pl.ds(0 if piece == 2 else SPAN, SPAN), lanes(piece)]
        dst = relay.at[1 if piece == 2 else 0, :, lanes(piece)]
        return copy(src, dst, far_send.at[piece], far_recv.at[piece], device)

    def from_relay(piece, device):
        src = relay.at[1 if piece == 2 else 0, :, lanes(piece)]
        chunk, sem = (CHUNKS - 2, CHUNKS - 2) if piece == 2 else (CHUNKS - 1, CHUNKS - 1 + piece)
        return copy(src, kvb.at[chunk, :, lanes(piece)], mid_send.at[piece], recv_sem.at[sem], device)

    relays = jnp.logical_or(far, mid)

    @pl.when(relays)
    def _():
        pl.semaphore_wait(barrier, 3)

    @pl.when(jnp.logical_not(relays))
    def _():
        pl.semaphore_wait(barrier, 2)

    @pl.when(far)
    def _():
        for piece in PIECES:
            to_relay(piece, at(i + 16 - FAR_Z + MID_Z)).start()

    def send_own(s):
        rows = kv_hbm.at[pl.ds(s * SPAN, SPAN)]
        chunk_copy(rows, 4 + s, ahead).start()
        chunk_copy(rows, 2 + s, above).start()

    send_own(0)

    local[0].wait()
    local[1].wait()
    row = lax.broadcasted_iota(jnp.int32, (16, 128), 0)
    note = jnp.zeros((16, 128), F32)
    for side in range(2):
        for g in range(4):
            e = exp_ref[side, g]
            note = jnp.where(row == 4 * side + g, jnp.where(e > 0, 2.0, jnp.where(e < 0, 0.5, 1.0)), note)
    for s in range(2):
        index = lax.div(pos_ref[s * SPAN], SPAN)
        note = jnp.where(row == 8 + 2 * s, lax.div(index, 32).astype(F32), note)
        note = jnp.where(row == 9 + 2 * s, lax.rem(index, 32).astype(F32), note)
    notes[0] = note.astype(BF16)
    note_copy(notes.at[0], 2, ahead).start()
    note_copy(notes.at[0], 1, above).start()
    send_own(1)

    late = z < 3
    turns = {
        4: jnp.where(late, 4, 2),
        5: jnp.where(late, 5, 3),
        6: jnp.where(late, 6, 5),
        7: jnp.where(z > 10, 6, 7),
    }

    def arrive(chunk):
        chunk_copy(kvb.at[chunk], chunk, ahead).wait_recv()

    def exchange(t):
        for piece in PIECES:
            @pl.when(jnp.logical_and(mid, t == MID_TURNS[piece]))
            def _(piece=piece):
                to_relay(piece, ahead).wait_recv()
                from_relay(piece, at(i - MID_Z)).start()

        for chunk, turn in turns.items():
            @pl.when(t == turn)
            def _(chunk=chunk):
                block = chunk // 2
                if chunk % 2 == 0:
                    note_copy(notes.at[block], block, ahead).wait_recv()
                    note_copy(notes.at[block], block + 1, ahead).start()
                arrive(chunk)
                if chunk < 6:
                    chunk_copy(kvb.at[chunk], chunk + 2, ahead).start()
                else:
                    @pl.when(jnp.logical_not(last))
                    def _():
                        if chunk == 6:
                            chunk_copy(kvb.at[chunk], chunk + 2, ahead).start()
                        else:
                            for side in range(2):
                                half_copy(kvb.at[chunk], side, ahead).start()

    local[4].wait()
    for h in range(HEADS):
        x = q_in[:, h * DIM : (h + 1) * DIM].astype(F32) * SCALE
        hi = x.astype(BF16)
        q2[h, :, 0:DIM] = hi
        q2[h, :, DIM : 2 * DIM] = (x - hi.astype(F32)).astype(BF16)
    mx[...] = jnp.full(mx.shape, -BIG, F32)
    acc[...] = jnp.zeros(acc.shape, F32)
    va[:, DIM : 2 * DIM] = jnp.ones((SPAN, DIM), BF16)

    def unpack(block, span, sides=(0, 1)):
        note = notes[block].astype(F32)

        def of(low, high):
            return jnp.where(span == 0, note[low : low + 1], note[high : high + 1])

        for g in range(2):
            rows = pl.ds(g * GROUP, GROUP)
            if 0 in sides:
                k = kvb[2 * block + span, rows, 0:DIM].astype(F32) * of(g, 2 + g)
                k = k.T.astype(BF16)
                kt[0:DIM, g * GROUP : (g + 1) * GROUP] = k
                kt[DIM : 2 * DIM, g * GROUP : (g + 1) * GROUP] = k
            if 1 in sides:
                v = kvb[2 * block + span, rows, DIM : 2 * DIM].astype(F32) * of(4 + g, 6 + g)
                va[rows, 0:DIM] = v.astype(BF16)
        return of(8, 10) * 32.0 + of(9, 11)

    def weigh(h, penalty):
        s = jnp.dot(q2[h], kt[...], preferred_element_type=F32)
        if penalty is None:
            s = s + bias[...]
        m_old = mx[h]
        m_new, p = [], []
        for r in range(2):
            rows = slice(r * SPAN, (r + 1) * SPAN)
            a, b = s[rows, 0:128], s[rows, 128:256]
            top = jnp.max(jnp.maximum(a, b), axis=1, keepdims=True)
            if penalty is None:
                m = jnp.maximum(m_old[rows], top)
                off = m
            else:
                m = jnp.maximum(m_old[rows], top - penalty[r])
                off = m + penalty[r]
            m_new.append(m)
            p.append(jnp.concatenate([jnp.exp2(a - off), jnp.exp2(b - off)], axis=1).astype(BF16))
        m_new = jnp.concatenate(m_new, axis=0)
        return m_new, jnp.exp2(m_old - m_new), jnp.concatenate(p, axis=0)

    def update(penalty):
        for h in range(HEADS):
            m_new, alpha, p = weigh(h, penalty)
            numer, total = gather(acc, va, h, alpha, p)
            mx[h] = m_new
            acc[h, :, 0:DIM] = numer
            acc[h, :, DIM : 2 * DIM] = total

    note = notes[0].astype(F32)
    mine = [note[8 + 2 * r : 9 + 2 * r] * 32.0 + note[9 + 2 * r : 10 + 2 * r] for r in range(2)]

    def penalties(place):
        return [jnp.where(place < mine[r], 0.0, BIG) for r in range(2)]

    local[2].wait()
    local[3].wait()

    def own_step(s, carry):
        place = unpack(0, s)
        row = lax.broadcasted_iota(jnp.int32, (SPAN, 128), 0)
        col = lax.broadcasted_iota(jnp.int32, (SPAN, 128), 1)
        for r in range(2):
            apart = (mine[r] - place) * SPAN
            for c in range(2):
                beyond = (row - col - c * 128).astype(F32) + apart
                bias[r * SPAN : (r + 1) * SPAN, c * 128 : (c + 1) * 128] = jnp.where(beyond >= 0, 0.0, -BIG)
        update(None)
        return carry

    lax.fori_loop(0, 2, own_step, 0)

    def step(t, carry):
        exchange(t)

        @pl.when(jnp.logical_or(t == 2, t == 8))
        def _():
            block = t // 2
            note_copy(notes.at[block], block, ahead).wait_recv()

        @pl.when(jnp.logical_or(t < 4, t == 8))
        def _():
            arrive(t)

        update(penalties(unpack(t // 2, lax.rem(t, 2))))
        return carry

    lax.fori_loop(2, CHUNKS - 1, step, 0)

    half_copy(kvb.at[CHUNKS - 1], 0, ahead).wait_recv()
    penalty = penalties(unpack(BLOCKS - 1, 1, (0,)))
    for h in range(HEADS):
        _, alpha, p = weigh(h, penalty)
        mx[h] = alpha
        weights[h] = p
    half_copy(kvb.at[CHUNKS - 1], 1, ahead).wait_recv()
    unpack(BLOCKS - 1, 1, (1,))

    for chunk in range(2, CHUNKS - 2):
        chunk_copy(kvb.at[chunk], chunk, ahead).wait_send()

    @pl.when(jnp.logical_not(last))
    def _():
        chunk_copy(kvb.at[CHUNKS - 2], CHUNKS - 2, ahead).wait_send()
        for side in range(2):
            half_copy(kvb.at[CHUNKS - 1], side, ahead).wait_send()

    @pl.when(far)
    def _():
        for piece in PIECES:
            to_relay(piece, ahead).wait_send()

    @pl.when(mid)
    def _():
        for piece in PIECES:
            from_relay(piece, ahead).wait_send()

    for block in range(1, BLOCKS):
        note_copy(notes.at[block], block, ahead).wait_send()


def solution(mesh):
    n_outer, n_inner = mesh.shape["outer"], mesh.shape["inner"]

    def local(queries, kv_codes, scale_exp, positions):
        tokens = queries.shape[0]
        in_hbm = pl.BlockSpec(memory_space=pltpu.HBM)
        operands = [queries, kv_codes, scale_exp.T, positions]
        in_vmem = pl.BlockSpec(memory_space=pltpu.VMEM)
        state = pl.pallas_call(
            functools.partial(kernel, n_outer, n_inner),
            out_shape=[
                pltpu.VMEM((HEADS, tokens, 2 * DIM), F32),
                pltpu.VMEM((HEADS, tokens, 128), F32),
                pltpu.VMEM((HEADS, tokens, SPAN), BF16),
                pltpu.VMEM((SPAN, 2 * DIM), BF16),
            ],
            in_specs=[in_hbm] * 4,
            out_specs=[in_vmem] * 4,
            scratch_shapes=[
                pltpu.SMEM((2, tokens // GROUP), jnp.int32),
                pltpu.SMEM((tokens,), jnp.int32),
                pltpu.VMEM((tokens, HEADS * DIM), BF16),
                pltpu.VMEM((CHUNKS, SPAN, 2 * DIM), BF16),
                pltpu.VMEM((BLOCKS, 16, 128), BF16),
                pltpu.VMEM((2, SPAN, 2 * DIM), BF16),
                pltpu.VMEM((HEADS, tokens, 2 * DIM), BF16),
                pltpu.VMEM((2 * DIM, SPAN), BF16),
                pltpu.VMEM((tokens, SPAN), F32),
                pltpu.SemaphoreType.DMA((5,)),
                pltpu.SemaphoreType.DMA((CHUNKS + 1,)),
                pltpu.SemaphoreType.DMA((CHUNKS + 1,)),
                pltpu.SemaphoreType.DMA((BLOCKS,)),
                pltpu.SemaphoreType.DMA((BLOCKS,)),
                pltpu.SemaphoreType.DMA((3,)),
                pltpu.SemaphoreType.DMA((3,)),
                pltpu.SemaphoreType.DMA((3,)),
            ],
            compiler_params=pltpu.CompilerParams(
                collective_id=0, has_side_effects=True, vmem_limit_bytes=32 * 2**20
            ),
            name="span_attention",
        )(*[pltpu.with_memory_space_constraint(x, pltpu.HBM) for x in operands])
        return pl.pallas_call(
            finish,
            out_shape=pltpu.HBM((tokens, HEADS * DIM), BF16),
            in_specs=[in_vmem] * 4,
            out_specs=in_hbm,
            scratch_shapes=[
                pltpu.VMEM((HEADS, tokens, DIM), BF16),
                pltpu.SemaphoreType.DMA((HEADS,)),
            ],
            compiler_params=pltpu.CompilerParams(vmem_limit_bytes=24 * 2**20),
            name="last_values",
        )(*state)

    split = P(("outer", "inner"), None)
    return jax.shard_map(
        local,
        mesh=mesh,
        in_specs=(split, split, split, P(("outer", "inner"))),
        out_specs=split,
        check_vma=False,
    )
```
